256 devices in a mesh: sens: 64 (over y, z_hi, x, core), beam: 4 (over z_lo).
Axes of the slice: x: 4, y: 4, z: 8 (z_hi: 2, z_lo: 4; z = z_hi * 4 + z_lo), core: 2. Of those that a mesh axis runs over, the one named last changes fastest.
Arguments:
- samples: bfloat16 [16384, 64, 1024], P('sens', 'beam'), may hold values from -6 to 6
- weights: bfloat16 [2, 32, 16384, 512], P(None, None, 'sens', 'beam'), may hold values from -0.046875 to 0.046875
- chosen_frequency_bins: int32 [32], replicated, may hold values from 1 to 511
Outputs:
- cross_spectra: float32 [2, 64, 512, 256], P(None, 'sens', 'beam')
The draws below stay inside these ranges and needn't reach their ends.
Inputs may be any that keep to these rules, and one draw needn't show every extreme that they name: `chosen_frequency_bins`: channel bins, possibly repeated.
All inputs are finite; a program needn't handle non-finite values.
Results may differ from the reference program's by a relative error of at most 0.0051.
Values may be sent and summed in bfloat16 or wider, within the bound.
No kernel may reach another device: no remote copies, remote signals or barrier semaphores. Data moves between devices by JAX's collectives and lax.ppermute only.
A program may use at most 128 MiB of HBM per device.

```python
import math
import jax
import jax.numpy as jnp
from jax import lax

S = 16384
NFFT = 1024
B = 512
SNAP = 64
CH = 32


def with_ends(drawn, rng, low, largest):
    dims = drawn.shape
    spot = [jax.random.randint(jax.random.fold_in(rng, axis), (), 0, dims[axis]) for axis in range(len(dims))]
    drawn = drawn.at[tuple(spot)].set(low)
    longest = dims.index(max(dims))
    spot[longest] = (spot[longest] + 1) % dims[longest]
    return drawn.at[tuple(spot)].set(largest)


def level_of(own_key, shape, split, least, high):
    level, own = 1.0, jax.random.fold_in(own_key, 6)
    for dim, shards_of in split:
        heights = jnp.exp(jax.random.uniform(jax.random.fold_in(own, dim), (shards_of,), jnp.float32, least / len(split), high / len(split)))
        level = level * jnp.repeat(heights, shape[dim] // shards_of).reshape([-1 if axis == dim else 1 for axis in range(len(shape))])
    return level


def gaussian(key, dims, spread, limit, cuts=(), kind=jnp.bfloat16):
    result = spread * jax.random.normal(key, dims, jnp.float32)
    if cuts:
        result = result * level_of(key, dims, cuts, -0.22, 0.18)
    return jnp.clip(result, -limit, limit).astype(kind)


def setup_inputs(seed: int = 0) -> dict:
    key_of = jax.random.split(jax.random.key(seed), 4)
    return {
        "samples": gaussian(key_of[0], (S, SNAP, NFFT), 1.0, 6.0, ((0, 64), (1, 4))),
        "weights": gaussian(key_of[1], (2, CH, S, B), S ** -0.5, 0.046875, ((2, 64), (3, 4))),
        "chosen_frequency_bins": with_ends(jax.random.randint(key_of[2], (CH,), 1, NFFT // 2), jax.random.fold_in(key_of[2], 1), 1, (NFFT // 2) - 1).astype(jnp.int32),
    }


def dft_table(chosen_frequency_bins, fourier_length):
    clock_ticks = jnp.arange(fourier_length, dtype=jnp.int32)
    rotation_radians = clock_ticks[:, None] * chosen_frequency_bins[None, :].astype(jnp.int32) % fourier_length
    angles = 2.0 * math.pi / fourier_length * rotation_radians.astype(jnp.float32)
    hann_envelope = 0.5 - 0.5 * jnp.cos(2.0 * math.pi / fourier_length * clock_ticks.astype(jnp.float32))
    scaling = (hann_envelope / math.sqrt(fourier_length))[:, None]
    return jnp.concatenate([scaling * jnp.cos(angles), -scaling * jnp.sin(angles)], axis=1).astype(jnp.bfloat16)

def contract(left, right):
    return lax.dot_general(left, right, (((0,), (0,)), ((), ())), precision=lax.Precision.HIGHEST, preferred_element_type=jnp.float32)

def reference(samples, weights, chosen_frequency_bins):
    table = dft_table(chosen_frequency_bins, NFFT)
    spectra = jnp.dot(samples.reshape(S * SNAP, NFFT), table, preferred_element_type=jnp.float32).astype(jnp.bfloat16)
    spectra = spectra.reshape(S, SNAP, 2, CH)
    inverse = 1.0 / SNAP

    def one_channel(index):
        column = lax.dynamic_index_in_dim(spectra, index, 3, keepdims=False)
        stacked = column.transpose(1, 2, 0).reshape(SNAP, 2 * S)
        weight_real = weights[0][index]
        imag_w = weights[1][index]
        upper = jnp.concatenate([weight_real, imag_w], axis=1)
        lower = jnp.concatenate([-imag_w, weight_real], axis=1)
        block = jnp.concatenate([upper, lower], axis=0)
        beamed = jnp.dot(stacked, block, preferred_element_type=jnp.float32)
        output_real = beamed[:, :B]
        imag_y = beamed[:, B:]
        real_g = (contract(output_real, output_real) + contract(imag_y, imag_y)) * inverse
        imag_g = (contract(imag_y, output_real) - contract(output_real, imag_y)) * inverse
        return jnp.stack([real_g, imag_g])
    grams = lax.map(one_channel, jnp.arange(CH, dtype=jnp.int32))
    grams = grams.reshape(CH, 2, B, 2, B // 2).transpose(1, 0, 3, 2, 4)
    return grams.reshape(2, CH * 2, B, B // 2)
```

```python
import math

import jax
import jax.numpy as jnp
from jax import lax
from jax.sharding import Mesh, PartitionSpec as P

AXES = ("y", "zh", "x", "core", "q")
NEAR = [(0, 1), (1, 0), (2, 3), (3, 2)]
MIDDLE = [(1, 2), (2, 1)]
FAR = [(0, 2), (2, 0), (1, 3), (3, 1)]
FORWARD = [(2, 3), (1, 0)]
SWAP = [(0, 1), (1, 0)]


def dft_table(chosen_frequency_bins, fourier_length):
    clock_ticks = jnp.arange(fourier_length, dtype=jnp.int32)
    rotation_radians = clock_ticks[:, None] * chosen_frequency_bins[None, :] % fourier_length
    angles = 2.0 * math.pi / fourier_length * rotation_radians.astype(jnp.float32)
    hann_envelope = 0.5 - 0.5 * jnp.cos(
        2.0 * math.pi / fourier_length * clock_ticks.astype(jnp.float32)
    )
    scaling = (hann_envelope / math.sqrt(fourier_length))[:, None]
    return jnp.concatenate([scaling * jnp.cos(angles), -scaling * jnp.sin(angles)], axis=1).astype(
        jnp.bfloat16
    )


def contract(left, right):
    return lax.dot_general(
        left,
        right,
        (((0,), (0,)), ((), ())),
        precision=lax.Precision.HIGHEST,
        preferred_element_type=jnp.float32,
    )


def local(samples, weights, chosen_frequency_bins):
    sens_local, snap_local, fourier_length = samples.shape
    chans = chosen_frequency_bins.shape[0]
    beams_local = weights.shape[3]
    core = lax.axis_index("core")
    q = lax.axis_index("q")
    table = dft_table(chosen_frequency_bins, fourier_length)
    spectra = jnp.dot(
        samples.reshape(sens_local * snap_local, fourier_length),
        table,
        preferred_element_type=jnp.float32,
    ).astype(jnp.bfloat16)
    spectra = spectra.reshape(sens_local, snap_local, 2, chans).transpose(2, 3, 1, 0)
    far = lax.ppermute(spectra, "q", FAR)
    near = lax.ppermute(spectra, "q", NEAR)
    middle = lax.ppermute(spectra, "q", MIDDLE)
    forward = lax.ppermute(far, "q", FORWARD)
    third = jnp.where((q == 1) | (q == 2), middle, forward)
    every = jnp.concatenate([spectra, near, far, third], axis=2)
    real_x, imag_x = every[0], every[1]
    form = "cns,csb->cnb"
    dot = lambda a, b: jnp.einsum(form, a, b, preferred_element_type=jnp.float32)
    real_y = dot(real_x, weights[0]) - dot(imag_x, weights[1])
    imag_y = dot(real_x, weights[1]) + dot(imag_x, weights[0])
    mine = jnp.where(core == 0, real_y, imag_y)
    other = jnp.where(core == 0, imag_y, real_y)
    snaps = mine.shape[1]
    mine = mine + lax.ppermute(other.astype(jnp.bfloat16), "core", SWAP).astype(jnp.float32)
    mine = (
        mine.reshape(4, 2, 4, snaps, beams_local)
        .transpose(0, 2, 1, 3, 4)
        .astype(jnp.bfloat16)
        .reshape(16, 2, snaps, beams_local)
    )
    mine = lax.all_to_all(mine, ("y", "x"), 0, 0)
    mine = jnp.sum(mine.astype(jnp.float32), axis=0)
    mine = jnp.broadcast_to(mine[:, None], (2, 4, snaps, beams_local)).reshape(
        8, snaps, beams_local
    )
    mine = lax.all_to_all(mine, ("zh", "q"), 0, 0).reshape(2, 4, snaps, beams_local)
    mine = mine[0] + mine[1]
    mine = mine.reshape(4, 4, snaps // 4, beams_local)
    mine = jnp.stack(
        [mine[b, jnp.array([k ^ b for k in range(4)])] for b in range(4)]
    ).reshape(4, snaps, beams_local)
    other = lax.ppermute(mine, "core", SWAP)
    real_y = jnp.where(core == 0, mine, other)
    imag_y = jnp.where(core == 0, other, mine)
    inverse = 1.0 / snaps
    rows = lambda a: lax.dynamic_index_in_dim(a, q, 0, keepdims=False)
    columns = lambda a: (
        lax.dynamic_slice_in_dim(a, 2 * core, 2, 0)
        .transpose(1, 0, 2)
        .reshape(snaps, 2 * beams_local)
    )
    left_real, left_imag = rows(real_y), rows(imag_y)
    right = jnp.concatenate([columns(real_y), columns(imag_y)], axis=0)
    real_g = contract(jnp.concatenate([left_real, left_imag], axis=0), right)
    imag_g = contract(jnp.concatenate([left_imag, -left_real], axis=0), right)
    return jnp.stack([real_g * inverse, imag_g * inverse])[:, None]


def solution(mesh):
    fine = Mesh(mesh.devices.reshape(4, 2, 4, 2, 4), AXES)
    sens = ("y", "zh", "x", "core")
    return jax.shard_map(
        local,
        mesh=fine,
        in_specs=(P(sens, "q", None), P(None, None, sens, "q"), P()),
        out_specs=P(None, sens, "q", None),
        check_vma=False,
    )
```

```python
import functools
import math

import jax
import jax.numpy as jnp
from jax import lax
from jax.experimental import pallas as pl
from jax.experimental.pallas import tpu as pltpu
from jax.sharding import Mesh, PartitionSpec as P

AXES = ("y", "zh", "x", "core", "q")
NEAR = [(0, 1), (1, 0), (2, 3), (3, 2)]
MIDDLE = [(1, 2), (2, 1)]
OUT = [(2, 3), (1, 0)]
SWAP = [(0, 1), (1, 0)]


def cosine(ticks, length):
    left = length // 4 - jnp.minimum(ticks, length - ticks)
    angle = left.astype(jnp.float32) * (2.0 * math.pi / length)
    square = angle * angle
    value = jnp.float32(-1.0 / math.factorial(11))
    for k in (9, 7, 5, 3, 1):
        value = value * square + (-1.0) ** (k // 2) / math.factorial(k)
    return value * angle


def dft_table(bins, length):
    chans = bins.shape[0]
    lanes = 128
    row = lax.broadcasted_iota(jnp.int32, (2 * chans, lanes), 0)
    turns = jnp.zeros((2 * chans, lanes), jnp.int32)
    for c in range(chans):
        turns = jnp.where(row % chans == c, bins[c], turns)
    turns = jnp.concatenate([turns] * (length // lanes), axis=1)
    clock_ticks = lax.broadcasted_iota(jnp.int32, turns.shape, 1)
    quarter = jnp.where(lax.broadcasted_iota(jnp.int32, turns.shape, 0) >= chans, length // 4, 0)
    turned = (clock_ticks * turns + quarter) & (length - 1)
    hann_envelope = 0.5 - 0.5 * cosine(clock_ticks, length)
    return (hann_envelope / math.sqrt(length) * cosine(turned, length)).astype(jnp.bfloat16)


def spectra_kernel(part, steps, bins_in, samples, out, held, rows, turned, bins, sems, bins_sem):
    sensors, snaps, ticks = held.shape
    columns = 2 * bins.shape[0]
    block = sensors // steps
    bins_copy = pltpu.make_async_copy(bins_in, bins, bins_sem)
    bins_copy.start()
    copies = []
    for i in range(steps):
        copy = pltpu.make_async_copy(
            samples.at[pl.ds(part * sensors + i * block, block)],
            held.at[pl.ds(i * block, block)],
            sems.at[i],
        )
        copy.start()
        copies.append(copy)
    bins_copy.wait()
    table = dft_table(bins, ticks)
    half = block // 2
    for i in range(steps):
        copies[i].wait()
        for j in range(2):
            first = i * block + j * half
            rows[pl.ds(first * snaps, half * snaps), :columns] = lax.dot_general(
                held[pl.ds(first, half)].reshape(half * snaps, ticks),
                table,
                (((1,), (1,)), ((), ())),
                preferred_element_type=jnp.float32,
            )
    for n in range(snaps):
        one = rows[pl.ds(n, sensors, stride=snaps), :].T[:columns]
        turned[pl.ds(n, columns, stride=snaps), :] = one
    out[...] = turned[...].astype(jnp.bfloat16).reshape(out.shape)


def spectra_of(samples, bins, part, parts):
    sensors, snaps, ticks = samples.shape
    sensors = sensors // parts
    columns = 2 * bins.shape[0]
    steps = 4
    return pl.pallas_call(
        functools.partial(spectra_kernel, part, steps),
        out_shape=jax.ShapeDtypeStruct((columns, snaps, sensors), jnp.bfloat16),
        in_specs=[pl.BlockSpec(memory_space=pl.ANY)] * 2,
        out_specs=pl.BlockSpec(memory_space=pltpu.VMEM),
        scratch_shapes=[
            pltpu.VMEM((sensors, snaps, ticks), jnp.bfloat16),
            pltpu.VMEM((sensors * snaps, 128), jnp.float32),
            pltpu.VMEM((columns * snaps, sensors), jnp.float32),
            pltpu.SMEM(bins.shape, bins.dtype),
            pltpu.SemaphoreType.DMA((steps,)),
            pltpu.SemaphoreType.DMA(()),
        ],
        compiler_params=pltpu.CompilerParams(vmem_limit_bytes=55 * 2**20),
        cost_estimate=pl.CostEstimate(
            flops=2 * sensors * snaps * ticks * columns,
            bytes_accessed=2 * sensors * snaps * (ticks + columns),
            transcendentals=0,
        ),
        name="spectra",
    )(bins, samples)


def load_kernel(weights, out, sems):
    beams = weights.shape[3]
    copies = []
    for part in range(2):
        for i in range(2):
            half = weights.shape[1] // 2
            channels = pl.ds(i * half, half)
            copy = pltpu.make_async_copy(
                weights.at[part, channels],
                out.at[channels, :, pl.ds(part * beams, beams)],
                sems.at[part, i],
            )
            copy.start()
            copies.append(copy)
    for copy in copies:
        copy.wait()


def load(weights):
    _, chans, sensors, beams = weights.shape
    return pl.pallas_call(
        load_kernel,
        out_shape=jax.ShapeDtypeStruct((chans, sensors, 2 * beams), weights.dtype),
        in_specs=[pl.BlockSpec(memory_space=pl.ANY)],
        out_specs=pl.BlockSpec(memory_space=pltpu.VMEM),
        scratch_shapes=[pltpu.SemaphoreType.DMA((2, 2))],
        compiler_params=pltpu.CompilerParams(vmem_limit_bytes=48 * 2**20),
        cost_estimate=pl.CostEstimate(
            flops=0, bytes_accessed=2 * weights.size * 2, transcendentals=0
        ),
        name="load",
    )(weights)


def beams_kernel(place, *refs):
    weights, keep, send = refs[-3:]
    own, near, middle, out, middle_2, out_2 = [refs[2 * k : 2 * k + 2] for k in range(6)]
    second = place[1] == 1
    orders = (
        (own, near, out, out_2),
        (near, own, middle, middle_2),
        (middle_2, middle, own, near),
        (out_2, out, near, own),
    )

    def run(order):
        def one_channel(ch, _):
            left = []
            for part in range(2):
                for one, two in order:
                    left.append(jnp.concatenate([one[part, ch], two[part, ch]], axis=1))
            left = jnp.concatenate(left, axis=0)
            both = jnp.dot(left, weights[ch], preferred_element_type=jnp.float32)
            half, beams = both.shape[0] // 2, both.shape[1] // 2
            real_y = both[:half, :beams] - both[half:, beams:]
            imag_y = both[:half, beams:] + both[half:, :beams]
            to = (ch // 8 * 4 + ch % 4, ch // 4 % 2)
            keep[to] = jnp.where(second, imag_y, real_y)
            send[to] = jnp.where(second, real_y, imag_y).astype(jnp.bfloat16)
            return 0

        lax.fori_loop(0, weights.shape[0], one_channel, 0, unroll=8)

    for q in range(4):
        pl.when(place[0] == q)(functools.partial(run, orders[q]))


def partial_beams(place, blocks, weights):
    _, chans, snaps, sensors = blocks[0].shape
    beams = weights.shape[2] // 2
    shape = (chans // 2, 2, 4 * snaps, beams)
    return pl.pallas_call(
        beams_kernel,
        out_shape=[
            jax.ShapeDtypeStruct(shape, jnp.float32),
            jax.ShapeDtypeStruct(shape, jnp.bfloat16),
        ],
        in_specs=[pl.BlockSpec(memory_space=pltpu.SMEM)]
        + [pl.BlockSpec(memory_space=pltpu.VMEM)] * (len(blocks) + 1),
        out_specs=[pl.BlockSpec(memory_space=pltpu.VMEM)] * 2,
        compiler_params=pltpu.CompilerParams(vmem_limit_bytes=32 * 2**20),
        name="beams",
    )(place, *blocks, weights)


def gram_kernel(place, mine, other, out):
    q, core = place[0], place[1]
    snaps = mine.shape[2]
    whole = []
    for part in range(2):
        blocks = []
        for b in range(4):
            ours = mine[0, b].astype(jnp.float32) + mine[1, b].astype(jnp.float32)
            theirs = other[0, b].astype(jnp.float32) + other[1, b].astype(jnp.float32)
            blocks.append(jnp.where(core == part, ours, theirs))
        whole.append(blocks)
    real_y, imag_y = whole

    def row(a):
        low = jnp.where(q % 2 == 0, a[0], a[1])
        high = jnp.where(q % 2 == 0, a[2], a[3])
        return jnp.where(q < 2, low, high)

    def columns(a):
        return jnp.concatenate(
            [jnp.where(core == 0, a[0], a[2]), jnp.where(core == 0, a[1], a[3])], axis=1
        )

    left_real, left_imag = row(real_y), row(imag_y)
    right = jnp.concatenate([columns(real_y), columns(imag_y)], axis=0)
    inverse = 1.0 / snaps

    def contract(left):
        return lax.dot_general(
            left,
            right,
            (((0,), (0,)), ((), ())),
            precision=lax.Precision.HIGHEST,
            preferred_element_type=jnp.float32,
        )

    out[0, 0] = contract(jnp.concatenate([left_real, left_imag], axis=0)) * inverse
    out[1, 0] = contract(jnp.concatenate([left_imag, -left_real], axis=0)) * inverse


def gram(place, mine, other):
    beams = mine.shape[3]
    return pl.pallas_call(
        gram_kernel,
        out_shape=jax.ShapeDtypeStruct((2, 1, beams, 2 * beams), jnp.float32),
        in_specs=[
            pl.BlockSpec(memory_space=pltpu.SMEM),
            pl.BlockSpec(memory_space=pltpu.VMEM),
            pl.BlockSpec(memory_space=pltpu.VMEM),
        ],
        out_specs=pl.BlockSpec(memory_space=pltpu.VMEM),
        compiler_params=pltpu.CompilerParams(vmem_limit_bytes=32 * 2**20),
        name="gram",
    )(place, mine, other)


def local(samples, weights, chosen_frequency_bins):
    chans = chosen_frequency_bins.shape[0]
    place = jnp.stack([lax.axis_index("q"), lax.axis_index("core")]).astype(jnp.int32)
    own = [spectra_of(samples, chosen_frequency_bins, part, 2) for part in range(2)]
    own = [x.reshape(2, chans, *x.shape[1:]) for x in own]

    def pass_on(pieces, pairs):
        return [lax.ppermute(x, "q", pairs) for x in pieces]

    def after(piece, other):
        return lax.optimization_barrier((piece, other))[0]

    near = pass_on(own, NEAR)
    middle = pass_on(own, MIDDLE)
    out = pass_on(middle, OUT)
    middle_2 = pass_on(near, MIDDLE)
    out_2 = pass_on(middle_2, OUT)
    weights = load(after(weights, middle[0]))
    blocks = own + near + middle + out + middle_2 + out_2
    keep, send = partial_beams(place, blocks, weights)
    theirs = lax.ppermute(send, "core", SWAP)
    mine = (keep + theirs.astype(jnp.float32)).astype(jnp.bfloat16)
    mine = lax.all_to_all(mine, ("y", "x"), 0, 0)
    mine = jnp.sum(mine.astype(jnp.float32), axis=0).astype(jnp.bfloat16)
    mine = jnp.broadcast_to(mine[:, None], (2, 4, *mine.shape[1:]))
    mine = mine.reshape(8, *mine.shape[2:])
    mine = lax.all_to_all(mine, ("zh", "q"), 0, 0)
    mine = mine.reshape(2, 4, *mine.shape[1:])
    other = lax.ppermute(mine, "core", SWAP)
    return gram(place, mine, other)


def solution(mesh):
    fine = Mesh(mesh.devices.reshape(4, 2, 4, 2, 4), AXES)
    sens = ("y", "zh", "x", "core")
    return jax.shard_map(
        local,
        mesh=fine,
        in_specs=(P(sens, "q", None), P(None, None, sens, "q"), P()),
        out_specs=P(None, sens, "q", None),
        check_vma=False,
    )
```

```python
import functools
import math

import jax
import jax.numpy as jnp
from jax import lax
from jax.experimental import pallas as pl
from jax.experimental.pallas import tpu as pltpu
from jax.sharding import Mesh, PartitionSpec as P

AXES = ("y", "zh", "x", "core", "q")
NEAR = [(0, 1), (1, 0), (2, 3), (3, 2)]
MIDDLE = [(1, 2), (2, 1)]
FAR = [(0, 2), (2, 0), (1, 3), (3, 1)]
OUT = [(2, 3), (1, 0)]
SWAP = [(0, 1), (1, 0)]


def cosine(ticks, length):
    left = length // 4 - jnp.minimum(ticks, length - ticks)
    angle = left.astype(jnp.float32) * (2.0 * math.pi / length)
    square = angle * angle
    value = jnp.float32(-1.0 / math.factorial(11))
    for k in (9, 7, 5, 3, 1):
        value = value * square + (-1.0) ** (k // 2) / math.factorial(k)
    return value * angle


def dft_table(bins, length):
    chans = bins.shape[0]
    lanes = 128
    row = lax.broadcasted_iota(jnp.int32, (2 * chans, lanes), 0)
    turns = jnp.zeros((2 * chans, lanes), jnp.int32)
    for c in range(chans):
        turns = jnp.where(row % chans == c, bins[c], turns)
    turns = jnp.concatenate([turns] * (length // lanes), axis=1)
    clock_ticks = lax.broadcasted_iota(jnp.int32, turns.shape, 1)
    quarter = jnp.where(lax.broadcasted_iota(jnp.int32, turns.shape, 0) >= chans, length // 4, 0)
    turned = (clock_ticks * turns + quarter) & (length - 1)
    hann_envelope = 0.5 - 0.5 * cosine(clock_ticks, length)
    return (hann_envelope / math.sqrt(length) * cosine(turned, length)).astype(jnp.bfloat16)


def spectra_kernel(part, steps, bins_in, samples, out, held, rows, turned, bins, sems, bins_sem):
    sensors, snaps, ticks = held.shape
    columns = 2 * bins.shape[0]
    block = sensors // steps
    bins_copy = pltpu.make_async_copy(bins_in, bins, bins_sem)
    bins_copy.start()
    copies = []
    for i in range(steps):
        copy = pltpu.make_async_copy(
            samples.at[pl.ds(part * sensors + i * block, block)],
            held.at[pl.ds(i * block, block)],
            sems.at[i],
        )
        copy.start()
        copies.append(copy)
    bins_copy.wait()
    table = dft_table(bins, ticks)
    half = block // 2
    for i in range(steps):
        copies[i].wait()
        for j in range(2):
            first = i * block + j * half
            rows[pl.ds(first * snaps, half * snaps), :columns] = lax.dot_general(
                held[pl.ds(first, half)].reshape(half * snaps, ticks),
                table,
                (((1,), (1,)), ((), ())),
                preferred_element_type=jnp.float32,
            )
    for n in range(snaps):
        one = rows[pl.ds(n, sensors, stride=snaps), :].T[:columns]
        turned[pl.ds(n, columns, stride=snaps), :] = one
    out[...] = turned[...].astype(jnp.bfloat16).reshape(out.shape)


def spectra_of(samples, bins, part, parts):
    sensors, snaps, ticks = samples.shape
    sensors = sensors // parts
    columns = 2 * bins.shape[0]
    steps = 4
    return pl.pallas_call(
        functools.partial(spectra_kernel, part, steps),
        out_shape=jax.ShapeDtypeStruct((columns, snaps, sensors), jnp.bfloat16),
        in_specs=[pl.BlockSpec(memory_space=pl.ANY)] * 2,
        out_specs=pl.BlockSpec(memory_space=pltpu.VMEM),
        scratch_shapes=[
            pltpu.VMEM((sensors, snaps, ticks), jnp.bfloat16),
            pltpu.VMEM((sensors * snaps, 128), jnp.float32),
            pltpu.VMEM((columns * snaps, sensors), jnp.float32),
            pltpu.SMEM(bins.shape, bins.dtype),
            pltpu.SemaphoreType.DMA((steps,)),
            pltpu.SemaphoreType.DMA(()),
        ],
        compiler_params=pltpu.CompilerParams(vmem_limit_bytes=55 * 2**20),
        cost_estimate=pl.CostEstimate(
            flops=2 * sensors * snaps * ticks * columns,
            bytes_accessed=2 * sensors * snaps * (ticks + columns),
            transcendentals=0,
        ),
        name="spectra",
    )(bins, samples)


def load_kernel(weights, out, sems):
    beams = weights.shape[3]
    copies = []
    for part in range(2):
        for i in range(2):
            half = weights.shape[1] // 2
            channels = pl.ds(i * half, half)
            copy = pltpu.make_async_copy(
                weights.at[part, channels],
                out.at[channels, :, pl.ds(part * beams, beams)],
                sems.at[part, i],
            )
            copy.start()
            copies.append(copy)
    for copy in copies:
        copy.wait()


def load(weights):
    _, chans, sensors, beams = weights.shape
    return pl.pallas_call(
        load_kernel,
        out_shape=jax.ShapeDtypeStruct((chans, sensors, 2 * beams), weights.dtype),
        in_specs=[pl.BlockSpec(memory_space=pl.ANY)],
        out_specs=pl.BlockSpec(memory_space=pltpu.VMEM),
        scratch_shapes=[pltpu.SemaphoreType.DMA((2, 2))],
        compiler_params=pltpu.CompilerParams(vmem_limit_bytes=48 * 2**20),
        cost_estimate=pl.CostEstimate(
            flops=0, bytes_accessed=2 * weights.size * 2, transcendentals=0
        ),
        name="load",
    )(weights)


def beams_kernel(place, *refs):
    weights, keep, send = refs[-3:]
    own, near, far, middle, out = [refs[2 * k : 2 * k + 2] for k in range(5)]
    second = place[1] == 1
    orders = (
        (own, near, far, out),
        (near, own, middle, far),
        (far, middle, own, near),
        (out, far, near, own),
    )

    def run(order):
        def one_channel(ch, _):
            left = []
            for part in range(2):
                for one, two in order:
                    left.append(jnp.concatenate([one[part, ch], two[part, ch]], axis=1))
            left = jnp.concatenate(left, axis=0)
            both = jnp.dot(left, weights[ch], preferred_element_type=jnp.float32)
            half, beams = both.shape[0] // 2, both.shape[1] // 2
            real_y = both[:half, :beams] - both[half:, beams:]
            imag_y = both[:half, beams:] + both[half:, :beams]
            to = (ch // 8 * 4 + ch % 4, ch // 4 % 2)
            keep[to] = jnp.where(second, imag_y, real_y)
            send[to] = jnp.where(second, real_y, imag_y).astype(jnp.bfloat16)
            return 0

        lax.fori_loop(0, weights.shape[0], one_channel, 0, unroll=8)

    for q in range(4):
        pl.when(place[0] == q)(functools.partial(run, orders[q]))


def partial_beams(place, blocks, weights):
    _, chans, snaps, sensors = blocks[0].shape
    beams = weights.shape[2] // 2
    shape = (chans // 2, 2, 4 * snaps, beams)
    return pl.pallas_call(
        beams_kernel,
        out_shape=[
            jax.ShapeDtypeStruct(shape, jnp.float32),
            jax.ShapeDtypeStruct(shape, jnp.bfloat16),
        ],
        in_specs=[pl.BlockSpec(memory_space=pltpu.SMEM)]
        + [pl.BlockSpec(memory_space=pltpu.VMEM)] * (len(blocks) + 1),
        out_specs=[pl.BlockSpec(memory_space=pltpu.VMEM)] * 2,
        compiler_params=pltpu.CompilerParams(vmem_limit_bytes=32 * 2**20),
        name="beams",
    )(place, *blocks, weights)


def gram_kernel(place, mine, other, out):
    q, core = place[0], place[1]
    snaps = mine.shape[2]
    whole = []
    for part in range(2):
        blocks = []
        for b in range(4):
            ours = mine[b, 0].astype(jnp.float32) + mine[b, 1].astype(jnp.float32)
            theirs = other[b, 0].astype(jnp.float32) + other[b, 1].astype(jnp.float32)
            blocks.append(jnp.where(core == part, ours, theirs))
        whole.append(blocks)
    real_y, imag_y = whole

    def row(a):
        low = jnp.where(q % 2 == 0, a[0], a[1])
        high = jnp.where(q % 2 == 0, a[2], a[3])
        return jnp.where(q < 2, low, high)

    def columns(a):
        return jnp.concatenate(
            [jnp.where(core == 0, a[0], a[2]), jnp.where(core == 0, a[1], a[3])], axis=1
        )

    left_real, left_imag = row(real_y), row(imag_y)
    right = jnp.concatenate([columns(real_y), columns(imag_y)], axis=0)
    inverse = 1.0 / snaps

    def contract(left):
        return lax.dot_general(
            left,
            right,
            (((0,), (0,)), ((), ())),
            precision=lax.Precision.HIGHEST,
            preferred_element_type=jnp.float32,
        )

    out[0, 0] = contract(jnp.concatenate([left_real, left_imag], axis=0)) * inverse
    out[1, 0] = contract(jnp.concatenate([left_imag, -left_real], axis=0)) * inverse


def gram(place, mine, other):
    beams = mine.shape[3]
    return pl.pallas_call(
        gram_kernel,
        out_shape=jax.ShapeDtypeStruct((2, 1, beams, 2 * beams), jnp.float32),
        in_specs=[
            pl.BlockSpec(memory_space=pltpu.SMEM),
            pl.BlockSpec(memory_space=pltpu.VMEM),
            pl.BlockSpec(memory_space=pltpu.VMEM),
        ],
        out_specs=pl.BlockSpec(memory_space=pltpu.VMEM),
        compiler_params=pltpu.CompilerParams(vmem_limit_bytes=32 * 2**20),
        name="gram",
    )(place, mine, other)


def local(samples, weights, chosen_frequency_bins):
    chans = chosen_frequency_bins.shape[0]
    place = jnp.stack([lax.axis_index("q"), lax.axis_index("core")]).astype(jnp.int32)
    own = [spectra_of(samples, chosen_frequency_bins, part, 2) for part in range(2)]
    own = [x.reshape(2, chans, *x.shape[1:]) for x in own]

    def pass_on(pieces, pairs):
        return [lax.ppermute(x, "q", pairs) for x in pieces]

    def after(piece, other):
        return lax.optimization_barrier((piece, other))[0]

    far = pass_on(own, FAR)
    near = pass_on(own, NEAR)
    out = pass_on(far, OUT)
    middle = pass_on([after(x, far[0]) for x in own], MIDDLE)
    weights = load(after(weights, far[-1]))
    blocks = own + near + far + middle + out
    keep, send = partial_beams(place, blocks, weights)
    theirs = lax.ppermute(send, "core", SWAP)
    mine = (keep + theirs.astype(jnp.float32)).astype(jnp.bfloat16)
    mine = lax.all_to_all(mine, ("y", "x"), 0, 0)
    mine = jnp.sum(mine.astype(jnp.float32), axis=0).astype(jnp.bfloat16)
    mine = jnp.broadcast_to(mine[None], (4, 2, *mine.shape[1:]))
    mine = mine.reshape(8, *mine.shape[2:])
    mine = lax.all_to_all(mine, ("q", "zh"), 0, 0)
    mine = mine.reshape(4, 2, *mine.shape[1:])
    other = lax.ppermute(mine, "core", SWAP)
    return gram(place, mine, other)


def solution(mesh):
    fine = Mesh(mesh.devices.reshape(4, 2, 4, 2, 4), AXES)
    sens = ("y", "zh", "x", "core")
    return jax.shard_map(
        local,
        mesh=fine,
        in_specs=(P(sens, "q", None), P(None, None, sens, "q"), P()),
        out_specs=P(None, sens, "q", None),
        check_vma=False,
    )
```

```python
import functools
import math

import jax
import jax.numpy as jnp
from jax import lax
from jax.experimental import pallas as pl
from jax.experimental.pallas import tpu as pltpu
from jax.sharding import Mesh, PartitionSpec as P

AXES = ("y", "zh", "x", "core", "q")
NEAR = [(0, 1), (1, 0), (2, 3), (3, 2)]
MIDDLE = [(1, 2), (2, 1)]
FAR = [(0, 2), (2, 0), (1, 3), (3, 1)]
OUT = [(2, 3), (1, 0)]
SWAP = [(0, 1), (1, 0)]


def cosine(ticks, length):
    left = length // 4 - jnp.minimum(ticks, length - ticks)
    angle = left.astype(jnp.float32) * (2.0 * math.pi / length)
    square = angle * angle
    value = jnp.float32(-1.0 / math.factorial(11))
    for k in (9, 7, 5, 3, 1):
        value = value * square + (-1.0) ** (k // 2) / math.factorial(k)
    return value * angle


def dft_table(bins, length):
    chans = bins.shape[0]
    lanes = 128
    row = lax.broadcasted_iota(jnp.int32, (2 * chans, lanes), 0)
    turns = jnp.zeros((2 * chans, lanes), jnp.int32)
    for c in range(chans):
        turns = jnp.where(row % chans == c, bins[c], turns)
    turns = jnp.concatenate([turns] * (length // lanes), axis=1)
    clock_ticks = lax.broadcasted_iota(jnp.int32, turns.shape, 1)
    quarter = jnp.where(lax.broadcasted_iota(jnp.int32, turns.shape, 0) >= chans, length // 4, 0)
    turned = (clock_ticks * turns + quarter) & (length - 1)
    hann_envelope = 0.5 - 0.5 * cosine(clock_ticks, length)
    return (hann_envelope / math.sqrt(length) * cosine(turned, length)).astype(jnp.bfloat16)


def spectra_kernel(part, steps, bins_in, samples, out, held, rows, turned, bins, sems, bins_sem):
    sensors, snaps, ticks = held.shape
    columns = 2 * bins.shape[0]
    block = sensors // steps
    bins_copy = pltpu.make_async_copy(bins_in, bins, bins_sem)
    bins_copy.start()
    copies = []
    for i in range(steps):
        copy = pltpu.make_async_copy(
            samples.at[pl.ds(part * sensors + i * block, block)],
            held.at[pl.ds(i * block, block)],
            sems.at[i],
        )
        copy.start()
        copies.append(copy)
    bins_copy.wait()
    table = dft_table(bins, ticks)
    half = block // 2
    for i in range(steps):
        copies[i].wait()
        for j in range(2):
            first = i * block + j * half
            rows[pl.ds(first * snaps, half * snaps), :columns] = lax.dot_general(
                held[pl.ds(first, half)].reshape(half * snaps, ticks),
                table,
                (((1,), (1,)), ((), ())),
                preferred_element_type=jnp.float32,
            )
    for n in range(snaps):
        one = rows[pl.ds(n, sensors, stride=snaps), :].T[:columns]
        turned[pl.ds(n, columns, stride=snaps), :] = one
    out[...] = turned[...].astype(jnp.bfloat16).reshape(out.shape)


def spectra_of(samples, bins, part, parts):
    sensors, snaps, ticks = samples.shape
    sensors = sensors // parts
    columns = 2 * bins.shape[0]
    steps = 4
    return pl.pallas_call(
        functools.partial(spectra_kernel, part, steps),
        out_shape=jax.ShapeDtypeStruct((columns, snaps, sensors), jnp.bfloat16),
        in_specs=[pl.BlockSpec(memory_space=pl.ANY)] * 2,
        out_specs=pl.BlockSpec(memory_space=pltpu.VMEM),
        scratch_shapes=[
            pltpu.VMEM((sensors, snaps, ticks), jnp.bfloat16),
            pltpu.VMEM((sensors * snaps, 128), jnp.float32),
            pltpu.VMEM((columns * snaps, sensors), jnp.float32),
            pltpu.SMEM(bins.shape, bins.dtype),
            pltpu.SemaphoreType.DMA((steps,)),
            pltpu.SemaphoreType.DMA(()),
        ],
        compiler_params=pltpu.CompilerParams(vmem_limit_bytes=50 * 2**20),
        cost_estimate=pl.CostEstimate(
            flops=2 * sensors * snaps * ticks * columns,
            bytes_accessed=2 * sensors * snaps * (ticks + columns),
            transcendentals=0,
        ),
        name="spectra",
    )(bins, samples)


def load_kernel(weights, out, sems):
    beams = weights.shape[3]
    copies = []
    for part in range(2):
        for i in range(2):
            half = weights.shape[1] // 2
            channels = pl.ds(i * half, half)
            copy = pltpu.make_async_copy(
                weights.at[part, channels],
                out.at[channels, :, pl.ds(part * beams, beams)],
                sems.at[part, i],
            )
            copy.start()
            copies.append(copy)
    for copy in copies:
        copy.wait()


def load(weights):
    _, chans, sensors, beams = weights.shape
    return pl.pallas_call(
        load_kernel,
        out_shape=jax.ShapeDtypeStruct((chans, sensors, 2 * beams), weights.dtype),
        in_specs=[pl.BlockSpec(memory_space=pl.ANY)],
        out_specs=pl.BlockSpec(memory_space=pltpu.VMEM),
        scratch_shapes=[pltpu.SemaphoreType.DMA((2, 2))],
        compiler_params=pltpu.CompilerParams(vmem_limit_bytes=48 * 2**20),
        cost_estimate=pl.CostEstimate(
            flops=0, bytes_accessed=2 * weights.size * 2, transcendentals=0
        ),
        name="load",
    )(weights)


def beams_kernel(place, *refs):
    weights, keep, send = refs[-3:]
    own, near, far, middle, out = [refs[2 * k : 2 * k + 2] for k in range(5)]
    second = place[1] == 1
    orders = (
        (own, near, far, out),
        (near, own, middle, far),
        (far, middle, own, near),
        (out, far, near, own),
    )

    def run(order):
        def one_channel(ch, _):
            left = []
            for part in range(2):
                for one, two in order:
                    left.append(jnp.concatenate([one[part, ch], two[part, ch]], axis=1))
            left = jnp.concatenate(left, axis=0)
            both = jnp.dot(left, weights[ch], preferred_element_type=jnp.float32)
            half, beams = both.shape[0] // 2, both.shape[1] // 2
            real_y = both[:half, :beams] - both[half:, beams:]
            imag_y = both[:half, beams:] + both[half:, :beams]
            to = (ch // 8 * 4 + ch % 4, ch // 4 % 2)
            keep[to] = jnp.where(second, imag_y, real_y)
            send[to] = jnp.where(second, real_y, imag_y).astype(jnp.bfloat16)
            return 0

        lax.fori_loop(0, weights.shape[0], one_channel, 0, unroll=True)

    for q in range(4):
        pl.when(place[0] == q)(functools.partial(run, orders[q]))


def partial_beams(place, blocks, weights):
    _, chans, snaps, sensors = blocks[0].shape
    beams = weights.shape[2] // 2
    shape = (chans // 2, 2, 4 * snaps, beams)
    return pl.pallas_call(
        beams_kernel,
        out_shape=[
            jax.ShapeDtypeStruct(shape, jnp.float32),
            jax.ShapeDtypeStruct(shape, jnp.bfloat16),
        ],
        in_specs=[pl.BlockSpec(memory_space=pltpu.SMEM)]
        + [pl.BlockSpec(memory_space=pltpu.VMEM)] * (len(blocks) + 1),
        out_specs=[pl.BlockSpec(memory_space=pltpu.VMEM)] * 2,
        compiler_params=pltpu.CompilerParams(vmem_limit_bytes=32 * 2**20),
        name="beams",
    )(place, *blocks, weights)


def gram_kernel(place, mine, other, out):
    q, core = place[0], place[1]
    snaps = mine.shape[2]
    whole = []
    for part in range(2):
        blocks = []
        for b in range(4):
            ours = mine[b, 0].astype(jnp.float32) + mine[b, 1].astype(jnp.float32)
            theirs = other[b, 0].astype(jnp.float32) + other[b, 1].astype(jnp.float32)
            blocks.append(jnp.where(core == part, ours, theirs))
        whole.append(blocks)
    real_y, imag_y = whole

    def row(a):
        low = jnp.where(q % 2 == 0, a[0], a[1])
        high = jnp.where(q % 2 == 0, a[2], a[3])
        return jnp.where(q < 2, low, high)

    def columns(a):
        return jnp.concatenate(
            [jnp.where(core == 0, a[0], a[2]), jnp.where(core == 0, a[1], a[3])], axis=1
        )

    left_real, left_imag = row(real_y), row(imag_y)
    right = jnp.concatenate([columns(real_y), columns(imag_y)], axis=0)
    inverse = 1.0 / snaps

    def contract(left):
        return lax.dot_general(
            left,
            right,
            (((0,), (0,)), ((), ())),
            precision=lax.Precision.HIGHEST,
            preferred_element_type=jnp.float32,
        )

    out[0, 0] = contract(jnp.concatenate([left_real, left_imag], axis=0)) * inverse
    out[1, 0] = contract(jnp.concatenate([left_imag, -left_real], axis=0)) * inverse


def gram(place, mine, other):
    beams = mine.shape[3]
    return pl.pallas_call(
        gram_kernel,
        out_shape=jax.ShapeDtypeStruct((2, 1, beams, 2 * beams), jnp.float32),
        in_specs=[
            pl.BlockSpec(memory_space=pltpu.SMEM),
            pl.BlockSpec(memory_space=pltpu.VMEM),
            pl.BlockSpec(memory_space=pltpu.VMEM),
        ],
        out_specs=pl.BlockSpec(memory_space=pltpu.VMEM),
        compiler_params=pltpu.CompilerParams(vmem_limit_bytes=32 * 2**20),
        name="gram",
    )(place, mine, other)


def local(samples, weights, chosen_frequency_bins):
    chans = chosen_frequency_bins.shape[0]
    place = jnp.stack([lax.axis_index("q"), lax.axis_index("core")]).astype(jnp.int32)
    bins = pltpu.with_memory_space_constraint(chosen_frequency_bins, pltpu.HBM)
    samples = pltpu.with_memory_space_constraint(samples, pltpu.HBM)
    own = [spectra_of(samples, bins, part, 2) for part in range(2)]
    own = [x.reshape(2, chans, *x.shape[1:]) for x in own]

    def pass_on(pieces, pairs):
        return [lax.ppermute(x, "q", pairs) for x in pieces]

    def after(piece, other):
        return lax.optimization_barrier((piece, other))[0]

    far = pass_on(own, FAR)
    near = pass_on(own, NEAR)
    out = pass_on(far, OUT)
    middle = pass_on([after(x, far[0]) for x in own], MIDDLE)
    weights = load(after(weights, far[-1]))
    blocks = own + near + far + middle + out
    keep, send = partial_beams(place, blocks, weights)
    theirs = lax.ppermute(send, "core", SWAP)
    mine = (keep + theirs.astype(jnp.float32)).astype(jnp.bfloat16)
    mine = lax.all_to_all(mine, ("y", "x"), 0, 0)
    mine = jnp.sum(mine.astype(jnp.float32), axis=0).astype(jnp.bfloat16)
    mine = jnp.broadcast_to(mine[None], (4, 2, *mine.shape[1:]))
    mine = mine.reshape(8, *mine.shape[2:])
    mine = lax.all_to_all(mine, ("q", "zh"), 0, 0)
    mine = mine.reshape(4, 2, *mine.shape[1:])
    other = lax.ppermute(mine, "core", SWAP)
    return gram(place, mine, other)


def solution(mesh):
    fine = Mesh(mesh.devices.reshape(4, 2, 4, 2, 4), AXES)
    sens = ("y", "zh", "x", "core")
    return jax.shard_map(
        local,
        mesh=fine,
        in_specs=(P(sens, "q", None), P(None, None, sens, "q"), P()),
        out_specs=P(None, sens, "q", None),
        check_vma=False,
    )
```

```python
import functools
import math

import jax
import jax.numpy as jnp
from jax import lax
from jax.experimental import pallas as pl
from jax.experimental.pallas import tpu as pltpu
from jax.sharding import Mesh, PartitionSpec as P

AXES = ("y", "zh", "x", "core", "q")
NEAR = [(0, 1), (1, 0), (2, 3), (3, 2)]
MIDDLE = [(1, 2), (2, 1)]
FAR = [(0, 2), (2, 0), (1, 3), (3, 1)]
OUT = [(2, 3), (1, 0)]
SWAP = [(0, 1), (1, 0)]


def cosine(ticks, length):
    left = length // 4 - jnp.minimum(ticks, length - ticks)
    angle = left.astype(jnp.float32) * (2.0 * math.pi / length)
    square = angle * angle
    value = jnp.float32(-1.0 / math.factorial(11))
    for k in (9, 7, 5, 3, 1):
        value = value * square + (-1.0) ** (k // 2) / math.factorial(k)
    return value * angle


def dft_table(bins, length):
    chans = bins.shape[0]
    lanes = 128
    row = lax.broadcasted_iota(jnp.int32, (2 * chans, lanes), 0)
    turns = jnp.zeros((2 * chans, lanes), jnp.int32)
    for c in range(chans):
        turns = jnp.where(row % chans == c, bins[c], turns)
    turns = jnp.concatenate([turns] * (length // lanes), axis=1)
    clock_ticks = lax.broadcasted_iota(jnp.int32, turns.shape, 1)
    quarter = jnp.where(lax.broadcasted_iota(jnp.int32, turns.shape, 0) >= chans, length // 4, 0)
    turned = (clock_ticks * turns + quarter) & (length - 1)
    hann_envelope = 0.5 - 0.5 * cosine(clock_ticks, length)
    return (hann_envelope / math.sqrt(length) * cosine(turned, length)).astype(jnp.bfloat16)


def spectra_kernel(part, steps, bins_in, samples, out, held, rows, turned, bins, sems, bins_sem):
    sensors, snaps, ticks = held.shape
    columns = 2 * bins.shape[0]
    block = sensors // steps
    bins_copy = pltpu.make_async_copy(bins_in, bins, bins_sem)
    bins_copy.start()
    copies = []
    for i in range(steps):
        copy = pltpu.make_async_copy(
            samples.at[pl.ds(part * sensors + i * block, block)],
            held.at[pl.ds(i * block, block)],
            sems.at[i],
        )
        copy.start()
        copies.append(copy)
    bins_copy.wait()
    table = dft_table(bins, ticks)
    half = block // 2
    for i in range(steps):
        copies[i].wait()
        for j in range(2):
            first = i * block + j * half
            rows[pl.ds(first * snaps, half * snaps), :columns] = lax.dot_general(
                held[pl.ds(first, half)].reshape(half * snaps, ticks),
                table,
                (((1,), (1,)), ((), ())),
                preferred_element_type=jnp.float32,
            )
    for n in range(snaps):
        one = rows[pl.ds(n, sensors, stride=snaps), :].T[:columns]
        turned[pl.ds(n, columns, stride=snaps), :] = one
    out[...] = turned[...].astype(jnp.bfloat16).reshape(out.shape)


def spectra_of(samples, bins, part, parts):
    sensors, snaps, ticks = samples.shape
    sensors = sensors // parts
    columns = 2 * bins.shape[0]
    steps = 4
    return pl.pallas_call(
        functools.partial(spectra_kernel, part, steps),
        out_shape=jax.ShapeDtypeStruct((columns, snaps, sensors), jnp.bfloat16),
        in_specs=[pl.BlockSpec(memory_space=pl.ANY)] * 2,
        out_specs=pl.BlockSpec(memory_space=pltpu.VMEM),
        scratch_shapes=[
            pltpu.VMEM((sensors, snaps, ticks), jnp.bfloat16),
            pltpu.VMEM((sensors * snaps, 128), jnp.float32),
            pltpu.VMEM((columns * snaps, sensors), jnp.float32),
            pltpu.SMEM(bins.shape, bins.dtype),
            pltpu.SemaphoreType.DMA((steps,)),
            pltpu.SemaphoreType.DMA(()),
        ],
        compiler_params=pltpu.CompilerParams(vmem_limit_bytes=50 * 2**20),
        cost_estimate=pl.CostEstimate(
            flops=2 * sensors * snaps * ticks * columns,
            bytes_accessed=2 * sensors * snaps * (ticks + columns),
            transcendentals=0,
        ),
        name="spectra",
    )(bins, samples)


def load_kernel(weights, out, sems):
    beams = weights.shape[3]
    copies = []
    for part in range(2):
        for i in range(2):
            half = weights.shape[1] // 2
            channels = pl.ds(i * half, half)
            copy = pltpu.make_async_copy(
                weights.at[part, channels],
                out.at[channels, :, pl.ds(part * beams, beams)],
                sems.at[part, i],
            )
            copy.start()
            copies.append(copy)
    for copy in copies:
        copy.wait()


def load(weights):
    _, chans, sensors, beams = weights.shape
    return pl.pallas_call(
        load_kernel,
        out_shape=jax.ShapeDtypeStruct((chans, sensors, 2 * beams), weights.dtype),
        in_specs=[pl.BlockSpec(memory_space=pl.ANY)],
        out_specs=pl.BlockSpec(memory_space=pltpu.VMEM),
        scratch_shapes=[pltpu.SemaphoreType.DMA((2, 2))],
        compiler_params=pltpu.CompilerParams(vmem_limit_bytes=48 * 2**20),
        cost_estimate=pl.CostEstimate(
            flops=0, bytes_accessed=2 * weights.size * 2, transcendentals=0
        ),
        name="load",
    )(weights)


def beams_kernel(*refs):
    weights, keep, send = refs[-3:]
    own, near, far, middle, out = [refs[2 * k : 2 * k + 2] for k in range(5)]
    q_here = lax.axis_index("q")
    second = lax.axis_index("core") == 1
    orders = (
        (own, near, far, out),
        (near, own, middle, far),
        (far, middle, own, near),
        (out, far, near, own),
    )

    def run(order):
        def one_channel(ch, _):
            left = []
            for part in range(2):
                for one, two in order:
                    left.append(jnp.concatenate([one[part, ch], two[part, ch]], axis=1))
            left = jnp.concatenate(left, axis=0)
            both = jnp.dot(left, weights[ch], preferred_element_type=jnp.float32)
            half, beams = both.shape[0] // 2, both.shape[1] // 2
            real_y = both[:half, :beams] - both[half:, beams:]
            imag_y = both[:half, beams:] + both[half:, :beams]
            to = (ch // 8 * 4 + ch % 4, ch // 4 % 2)
            keep[to] = jnp.where(second, imag_y, real_y)
            send[to] = jnp.where(second, real_y, imag_y).astype(jnp.bfloat16)
            return 0

        lax.fori_loop(0, weights.shape[0], one_channel, 0, unroll=True)

    for q in range(4):
        pl.when(q_here == q)(functools.partial(run, orders[q]))


def partial_beams(blocks, weights):
    _, chans, snaps, sensors = blocks[0].shape
    beams = weights.shape[2] // 2
    shape = (chans // 2, 2, 4 * snaps, beams)
    return pl.pallas_call(
        beams_kernel,
        out_shape=[
            jax.ShapeDtypeStruct(shape, jnp.float32),
            jax.ShapeDtypeStruct(shape, jnp.bfloat16),
        ],
        in_specs=[pl.BlockSpec(memory_space=pltpu.VMEM)] * (len(blocks) + 1),
        out_specs=[pl.BlockSpec(memory_space=pltpu.VMEM)] * 2,
        compiler_params=pltpu.CompilerParams(vmem_limit_bytes=32 * 2**20),
        name="beams",
    )(*blocks, weights)


def gram_kernel(mine, other, out):
    q, core = lax.axis_index("q"), lax.axis_index("core")
    snaps = mine.shape[2]
    whole = []
    for part in range(2):
        blocks = []
        for b in range(4):
            ours = mine[b, 0].astype(jnp.float32) + mine[b, 1].astype(jnp.float32)
            theirs = other[b, 0].astype(jnp.float32) + other[b, 1].astype(jnp.float32)
            blocks.append(jnp.where(core == part, ours, theirs))
        whole.append(blocks)
    real_y, imag_y = whole

    def row(a):
        low = jnp.where(q % 2 == 0, a[0], a[1])
        high = jnp.where(q % 2 == 0, a[2], a[3])
        return jnp.where(q < 2, low, high)

    def columns(a):
        return jnp.concatenate(
            [jnp.where(core == 0, a[0], a[2]), jnp.where(core == 0, a[1], a[3])], axis=1
        )

    left_real, left_imag = row(real_y), row(imag_y)
    right = jnp.concatenate([columns(real_y), columns(imag_y)], axis=0)
    inverse = 1.0 / snaps

    def contract(left):
        return lax.dot_general(
            left,
            right,
            (((0,), (0,)), ((), ())),
            precision=lax.Precision.HIGHEST,
            preferred_element_type=jnp.float32,
        )

    out[0, 0] = contract(jnp.concatenate([left_real, left_imag], axis=0)) * inverse
    out[1, 0] = contract(jnp.concatenate([left_imag, -left_real], axis=0)) * inverse


def gram(mine, other):
    beams = mine.shape[3]
    return pl.pallas_call(
        gram_kernel,
        out_shape=jax.ShapeDtypeStruct((2, 1, beams, 2 * beams), jnp.float32),
        in_specs=[pl.BlockSpec(memory_space=pltpu.VMEM)] * 2,
        out_specs=pl.BlockSpec(memory_space=pltpu.VMEM),
        compiler_params=pltpu.CompilerParams(vmem_limit_bytes=32 * 2**20),
        name="gram",
    )(mine, other)


def local(samples, weights, chosen_frequency_bins):
    chans = chosen_frequency_bins.shape[0]
    bins = pltpu.with_memory_space_constraint(chosen_frequency_bins, pltpu.HBM)
    samples = pltpu.with_memory_space_constraint(samples, pltpu.HBM)
    own = [spectra_of(samples, bins, part, 2) for part in range(2)]
    own = [x.reshape(2, chans, *x.shape[1:]) for x in own]

    def pass_on(pieces, pairs):
        return [lax.ppermute(x, "q", pairs) for x in pieces]

    def after(piece, other):
        return lax.optimization_barrier((piece, other))[0]

    far = pass_on(own, FAR)
    near = pass_on(own, NEAR)
    out = pass_on(far, OUT)
    middle = pass_on([after(x, far[0]) for x in own], MIDDLE)
    weights = load(after(weights, far[-1]))
    blocks = own + near + far + middle + out
    keep, send = partial_beams(blocks, weights)
    theirs = lax.ppermute(send, "core", SWAP)
    mine = (keep + theirs.astype(jnp.float32)).astype(jnp.bfloat16)
    mine = lax.all_to_all(mine, ("y", "x"), 0, 0)
    mine = jnp.sum(mine.astype(jnp.float32), axis=0).astype(jnp.bfloat16)
    mine = jnp.broadcast_to(mine[None], (4, 2, *mine.shape[1:]))
    mine = mine.reshape(8, *mine.shape[2:])
    mine = lax.all_to_all(mine, ("q", "zh"), 0, 0)
    mine = mine.reshape(4, 2, *mine.shape[1:])
    other = lax.ppermute(mine, "core", SWAP)
    return gram(mine, other)


def solution(mesh):
    fine = Mesh(mesh.devices.reshape(4, 2, 4, 2, 4), AXES)
    sens = ("y", "zh", "x", "core")
    return jax.shard_map(
        local,
        mesh=fine,
        in_specs=(P(sens, "q", None), P(None, None, sens, "q"), P()),
        out_specs=P(None, sens, "q", None),
        check_vma=False,
    )
```

```python
import functools
import math

import jax
import jax.numpy as jnp
from jax import lax
from jax.experimental import pallas as pl
from jax.experimental.pallas import tpu as pltpu
from jax.sharding import Mesh, PartitionSpec as P

AXES = ("y", "zh", "x", "core", "q")
NEAR = [(0, 1), (1, 0), (2, 3), (3, 2)]
MIDDLE = [(1, 2), (2, 1)]
FAR = [(0, 2), (2, 0), (1, 3), (3, 1)]
OUT = [(2, 3), (1, 0)]
SWAP = [(0, 1), (1, 0)]


def cosine(ticks, length):
    left = length // 4 - jnp.minimum(ticks, length - ticks)
    angle = left.astype(jnp.float32) * (2.0 * math.pi / length)
    square = angle * angle
    value = jnp.float32(-1.0 / math.factorial(11))
    for k in (9, 7, 5, 3, 1):
        value = value * square + (-1.0) ** (k // 2) / math.factorial(k)
    return value * angle


def dft_table(bins, length):
    chans = bins.shape[0]
    lanes = 128
    row = lax.broadcasted_iota(jnp.int32, (2 * chans, lanes), 0)
    turns = jnp.zeros((2 * chans, lanes), jnp.int32)
    for c in range(chans):
        turns = jnp.where(row % chans == c, bins[c], turns)
    turns = jnp.concatenate([turns] * (length // lanes), axis=1)
    clock_ticks = lax.broadcasted_iota(jnp.int32, turns.shape, 1)
    quarter = jnp.where(lax.broadcasted_iota(jnp.int32, turns.shape, 0) >= chans, length // 4, 0)
    turned = (clock_ticks * turns + quarter) & (length - 1)
    hann_envelope = 0.5 - 0.5 * cosine(clock_ticks, length)
    return (hann_envelope / math.sqrt(length) * cosine(turned, length)).astype(jnp.bfloat16)


def spectra_kernel(part, steps, bins_in, samples, out, held, rows, turned, bins, sems, bins_sem):
    sensors, snaps, ticks = held.shape
    columns = 2 * bins.shape[0]
    block = sensors // steps
    bins_copy = pltpu.make_async_copy(bins_in, bins, bins_sem)
    bins_copy.start()
    copies = []
    for i in range(steps):
        copy = pltpu.make_async_copy(
            samples.at[pl.ds(part * sensors + i * block, block)],
            held.at[pl.ds(i * block, block)],
            sems.at[i],
        )
        copy.start()
        copies.append(copy)
    bins_copy.wait()
    table = dft_table(bins, ticks)
    half = block // 2
    for i in range(steps):
        copies[i].wait()
        for j in range(2):
            first = i * block + j * half
            rows[pl.ds(first * snaps, half * snaps), :columns] = lax.dot_general(
                held[pl.ds(first, half)].reshape(half * snaps, ticks),
                table,
                (((1,), (1,)), ((), ())),
                preferred_element_type=jnp.float32,
            )
    for n in range(snaps):
        one = rows[pl.ds(n, sensors, stride=snaps), :].T[:columns]
        turned[pl.ds(n, columns, stride=snaps), :] = one
    out[...] = turned[: columns * snaps].astype(jnp.bfloat16).reshape(out.shape)


def spectra_of(samples, bins, part, parts):
    sensors, snaps, ticks = samples.shape
    sensors = sensors // parts
    columns = 2 * bins.shape[0]
    steps = 4
    return pl.pallas_call(
        functools.partial(spectra_kernel, part, steps),
        out_shape=jax.ShapeDtypeStruct((columns, snaps, sensors), jnp.bfloat16),
        in_specs=[pl.BlockSpec(memory_space=pl.ANY)] * 2,
        out_specs=pl.BlockSpec(memory_space=pltpu.VMEM),
        scratch_shapes=[
            pltpu.VMEM((sensors, snaps, ticks), jnp.bfloat16),
            pltpu.VMEM(((sensors + 1) * snaps, 128), jnp.float32),
            pltpu.VMEM(((columns + 1) * snaps, sensors), jnp.float32),
            pltpu.SMEM(bins.shape, bins.dtype),
            pltpu.SemaphoreType.DMA((steps,)),
            pltpu.SemaphoreType.DMA(()),
        ],
        compiler_params=pltpu.CompilerParams(vmem_limit_bytes=50 * 2**20),
        cost_estimate=pl.CostEstimate(
            flops=2 * sensors * snaps * ticks * columns,
            bytes_accessed=2 * sensors * snaps * (ticks + columns),
            transcendentals=0,
        ),
        name="spectra",
    )(bins, samples)


def load_kernel(weights, out, sems):
    beams = weights.shape[3]
    copies = []
    for part in range(2):
        for i in range(2):
            half = weights.shape[1] // 2
            channels = pl.ds(i * half, half)
            copy = pltpu.make_async_copy(
                weights.at[part, channels],
                out.at[channels, :, pl.ds(part * beams, beams)],
                sems.at[part, i],
            )
            copy.start()
            copies.append(copy)
    for copy in copies:
        copy.wait()


def load(weights):
    _, chans, sensors, beams = weights.shape
    return pl.pallas_call(
        load_kernel,
        out_shape=jax.ShapeDtypeStruct((chans, sensors, 2 * beams), weights.dtype),
        in_specs=[pl.BlockSpec(memory_space=pl.ANY)],
        out_specs=pl.BlockSpec(memory_space=pltpu.VMEM),
        scratch_shapes=[pltpu.SemaphoreType.DMA((2, 2))],
        compiler_params=pltpu.CompilerParams(vmem_limit_bytes=48 * 2**20),
        cost_estimate=pl.CostEstimate(
            flops=0, bytes_accessed=2 * weights.size * 2, transcendentals=0
        ),
        name="load",
    )(weights)


def beams_kernel(*refs):
    weights, keep, send = refs[-3:]
    own, near, far, middle, out = [refs[2 * k : 2 * k + 2] for k in range(5)]
    q_here = lax.axis_index("q")
    second = lax.axis_index("core") == 1
    orders = (
        (own, near, far, out),
        (near, own, middle, far),
        (far, middle, own, near),
        (out, far, near, own),
    )

    def run(order):
        def one_channel(ch, _):
            left = []
            for part in range(2):
                for one, two in order:
                    left.append(jnp.concatenate([one[part, ch], two[part, ch]], axis=1))
            left = jnp.concatenate(left, axis=0)
            both = jnp.dot(left, weights[ch], preferred_element_type=jnp.float32)
            half, beams = both.shape[0] // 2, both.shape[1] // 2
            real_y = both[:half, :beams] - both[half:, beams:]
            imag_y = both[:half, beams:] + both[half:, :beams]
            to = (ch // 8 * 4 + ch % 4, ch // 4 % 2)
            keep[to] = jnp.where(second, imag_y, real_y)
            send[to] = jnp.where(second, real_y, imag_y).astype(jnp.bfloat16)
            return 0

        lax.fori_loop(0, weights.shape[0], one_channel, 0, unroll=True)

    for q in range(4):
        pl.when(q_here == q)(functools.partial(run, orders[q]))


def partial_beams(blocks, weights):
    _, chans, snaps, sensors = blocks[0].shape
    beams = weights.shape[2] // 2
    shape = (chans // 2, 2, 4 * snaps, beams)
    return pl.pallas_call(
        beams_kernel,
        out_shape=[
            jax.ShapeDtypeStruct(shape, jnp.float32),
            jax.ShapeDtypeStruct(shape, jnp.bfloat16),
        ],
        in_specs=[pl.BlockSpec(memory_space=pltpu.VMEM)] * (len(blocks) + 1),
        out_specs=[pl.BlockSpec(memory_space=pltpu.VMEM)] * 2,
        compiler_params=pltpu.CompilerParams(vmem_limit_bytes=32 * 2**20),
        name="beams",
    )(*blocks, weights)


def gram_kernel(mine, other, out):
    q, core = lax.axis_index("q"), lax.axis_index("core")
    snaps = mine.shape[2]
    whole = []
    for part in range(2):
        blocks = []
        for b in range(4):
            ours = mine[b, 0].astype(jnp.float32) + mine[b, 1].astype(jnp.float32)
            theirs = other[b, 0].astype(jnp.float32) + other[b, 1].astype(jnp.float32)
            blocks.append(jnp.where(core == part, ours, theirs))
        whole.append(blocks)
    real_y, imag_y = whole

    def row(a):
        low = jnp.where(q % 2 == 0, a[0], a[1])
        high = jnp.where(q % 2 == 0, a[2], a[3])
        return jnp.where(q < 2, low, high)

    def columns(a):
        return jnp.concatenate(
            [jnp.where(core == 0, a[0], a[2]), jnp.where(core == 0, a[1], a[3])], axis=1
        )

    left_real, left_imag = row(real_y), row(imag_y)
    right = jnp.concatenate([columns(real_y), columns(imag_y)], axis=0)
    inverse = 1.0 / snaps

    def contract(left):
        return lax.dot_general(
            left,
            right,
            (((0,), (0,)), ((), ())),
            precision=lax.Precision.HIGHEST,
            preferred_element_type=jnp.float32,
        )

    out[0, 0] = contract(jnp.concatenate([left_real, left_imag], axis=0)) * inverse
    out[1, 0] = contract(jnp.concatenate([left_imag, -left_real], axis=0)) * inverse


def gram(mine, other):
    beams = mine.shape[3]
    return pl.pallas_call(
        gram_kernel,
        out_shape=jax.ShapeDtypeStruct((2, 1, beams, 2 * beams), jnp.float32),
        in_specs=[pl.BlockSpec(memory_space=pltpu.VMEM)] * 2,
        out_specs=pl.BlockSpec(memory_space=pltpu.VMEM),
        compiler_params=pltpu.CompilerParams(vmem_limit_bytes=32 * 2**20),
        name="gram",
    )(mine, other)


def local(samples, weights, chosen_frequency_bins):
    chans = chosen_frequency_bins.shape[0]
    bins = pltpu.with_memory_space_constraint(chosen_frequency_bins, pltpu.HBM)
    samples = pltpu.with_memory_space_constraint(samples, pltpu.HBM)
    own = [spectra_of(samples, bins, part, 2) for part in range(2)]
    own = [x.reshape(2, chans, *x.shape[1:]) for x in own]

    def pass_on(pieces, pairs):
        return [lax.ppermute(x, "q", pairs) for x in pieces]

    def after(piece, other):
        return lax.optimization_barrier((piece, other))[0]

    far = pass_on(own, FAR)
    near = pass_on(own, NEAR)
    out = pass_on(far, OUT)
    middle = pass_on([after(x, far[0]) for x in own], MIDDLE)
    weights = load(after(weights, far[-1]))
    blocks = own + near + far + middle + out
    keep, send = partial_beams(blocks, weights)
    theirs = lax.ppermute(send, "core", SWAP)
    mine = (keep + theirs.astype(jnp.float32)).astype(jnp.bfloat16)
    mine = lax.all_to_all(mine, ("y", "x"), 0, 0)
    mine = jnp.sum(mine.astype(jnp.float32), axis=0).astype(jnp.bfloat16)
    mine = jnp.broadcast_to(mine[None], (4, 2, *mine.shape[1:]))
    mine = mine.reshape(8, *mine.shape[2:])
    mine = lax.all_to_all(mine, ("q", "zh"), 0, 0)
    mine = mine.reshape(4, 2, *mine.shape[1:])
    other = lax.ppermute(mine, "core", SWAP)
    return gram(mine, other)


def solution(mesh):
    fine = Mesh(mesh.devices.reshape(4, 2, 4, 2, 4), AXES)
    sens = ("y", "zh", "x", "core")
    return jax.shard_map(
        local,
        mesh=fine,
        in_specs=(P(sens, "q", None), P(None, None, sens, "q"), P()),
        out_specs=P(None, sens, "q", None),
        check_vma=False,
    )
```

```python
import functools
import math

import jax
import jax.numpy as jnp
from jax import lax
from jax.experimental import pallas as pl
from jax.experimental.pallas import tpu as pltpu
from jax.sharding import Mesh, PartitionSpec as P

AXES = ("y", "zh", "x", "core", "q")
NEAR = [(0, 1), (1, 0), (2, 3), (3, 2)]
MIDDLE = [(1, 2), (2, 1)]
FAR = [(0, 2), (2, 0), (1, 3), (3, 1)]
OUT = [(2, 3), (1, 0)]
SWAP = [(0, 1), (1, 0)]


def cosine(ticks, length):
    left = length // 4 - jnp.minimum(ticks, length - ticks)
    angle = left.astype(jnp.float32) * (2.0 * math.pi / length)
    square = angle * angle
    value = jnp.float32(-1.0 / math.factorial(11))
    for k in (9, 7, 5, 3, 1):
        value = value * square + (-1.0) ** (k // 2) / math.factorial(k)
    return value * angle


def dft_table(bins, length):
    chans = bins.shape[0]
    lanes = 128
    row = lax.broadcasted_iota(jnp.int32, (2 * chans, lanes), 0)
    turns = jnp.zeros((2 * chans, lanes), jnp.int32)
    for c in range(chans):
        turns = jnp.where(row % chans == c, bins[c], turns)
    turns = jnp.concatenate([turns] * (length // lanes), axis=1)
    clock_ticks = lax.broadcasted_iota(jnp.int32, turns.shape, 1)
    quarter = jnp.where(lax.broadcasted_iota(jnp.int32, turns.shape, 0) >= chans, length // 4, 0)
    turned = (clock_ticks * turns + quarter) & (length - 1)
    hann_envelope = 0.5 - 0.5 * cosine(clock_ticks, length)
    return (hann_envelope / math.sqrt(length) * cosine(turned, length)).astype(jnp.bfloat16)


def spectra_kernel(part, steps, bins_in, samples, out, held, rows, turned, bins, sems, bins_sem):
    sensors, snaps, ticks = held.shape
    columns = 2 * bins.shape[0]
    block = sensors // steps
    bins_copy = pltpu.make_async_copy(bins_in, bins, bins_sem)
    bins_copy.start()
    copies = []
    for i in range(steps):
        copy = pltpu.make_async_copy(
            samples.at[pl.ds(part * sensors + i * block, block)],
            held.at[pl.ds(i * block, block)],
            sems.at[i],
        )
        copy.start()
        copies.append(copy)
    bins_copy.wait()
    table = dft_table(bins, ticks)
    half = block // 2
    for i in range(steps):
        copies[i].wait()
        for j in range(2):
            first = i * block + j * half
            rows[pl.ds(first * snaps, half * snaps), :columns] = lax.dot_general(
                held[pl.ds(first, half)].reshape(half * snaps, ticks),
                table,
                (((1,), (1,)), ((), ())),
                preferred_element_type=jnp.float32,
            )
    for n in range(snaps):
        one = rows[pl.ds(n, sensors, stride=snaps), :].T[:columns]
        turned[pl.ds(n, columns, stride=snaps), :] = one
    out[...] = turned[: columns * snaps].astype(jnp.bfloat16).reshape(out.shape)


def spectra_of(samples, bins, part, parts):
    sensors, snaps, ticks = samples.shape
    sensors = sensors // parts
    columns = 2 * bins.shape[0]
    steps = 4
    return pl.pallas_call(
        functools.partial(spectra_kernel, part, steps),
        out_shape=jax.ShapeDtypeStruct((columns, snaps, sensors), jnp.bfloat16),
        in_specs=[pl.BlockSpec(memory_space=pl.ANY)] * 2,
        out_specs=pl.BlockSpec(memory_space=pltpu.VMEM),
        scratch_shapes=[
            pltpu.VMEM((sensors, snaps, ticks), jnp.bfloat16),
            pltpu.VMEM(((sensors + 1) * snaps, 128), jnp.float32),
            pltpu.VMEM(((columns + 1) * snaps, sensors), jnp.float32),
            pltpu.SMEM(bins.shape, bins.dtype),
            pltpu.SemaphoreType.DMA((steps,)),
            pltpu.SemaphoreType.DMA(()),
        ],
        compiler_params=pltpu.CompilerParams(vmem_limit_bytes=50 * 2**20),
        cost_estimate=pl.CostEstimate(
            flops=2 * sensors * snaps * ticks * columns,
            bytes_accessed=2 * sensors * snaps * (ticks + columns),
            transcendentals=0,
        ),
        name="spectra",
    )(bins, samples)


def load_kernel(weights, out, sems):
    beams = weights.shape[3]
    copies = []
    for part in range(2):
        for i in range(2):
            half = weights.shape[1] // 2
            channels = pl.ds(i * half, half)
            copy = pltpu.make_async_copy(
                weights.at[part, channels],
                out.at[channels, :, pl.ds(part * beams, beams)],
                sems.at[part, i],
            )
            copy.start()
            copies.append(copy)
    for copy in copies:
        copy.wait()


def load(weights):
    _, chans, sensors, beams = weights.shape
    return pl.pallas_call(
        load_kernel,
        out_shape=jax.ShapeDtypeStruct((chans, sensors, 2 * beams), weights.dtype),
        in_specs=[pl.BlockSpec(memory_space=pl.ANY)],
        out_specs=pl.BlockSpec(memory_space=pltpu.VMEM),
        scratch_shapes=[pltpu.SemaphoreType.DMA((2, 2))],
        compiler_params=pltpu.CompilerParams(vmem_limit_bytes=48 * 2**20),
        cost_estimate=pl.CostEstimate(
            flops=0, bytes_accessed=2 * weights.size * 2, transcendentals=0
        ),
        name="load",
    )(weights)


def beams_kernel(*refs):
    weights, keep, send = refs[-3:]
    own, near, far, middle, out = [refs[2 * k : 2 * k + 2] for k in range(5)]
    q_here = lax.axis_index("q")
    second = lax.axis_index("core") == 1
    orders = (
        (own, near, far, out),
        (near, own, middle, far),
        (far, middle, own, near),
        (out, far, near, own),
    )

    def run(order):
        def one_channel(ch, _):
            left = []
            for part in range(2):
                for one, two in order:
                    left.append(jnp.concatenate([one[part, ch], two[part, ch]], axis=1))
            left = jnp.concatenate(left, axis=0)
            both = jnp.dot(left, weights[ch], preferred_element_type=jnp.float32)
            half, beams = both.shape[0] // 2, both.shape[1] // 2
            real_y = both[:half, :beams] - both[half:, beams:]
            imag_y = both[:half, beams:] + both[half:, :beams]
            to = (ch // 8 * 4 + ch % 4, ch // 4 % 2)
            keep[to] = jnp.where(second, imag_y, real_y)
            send[to] = jnp.where(second, real_y, imag_y).astype(jnp.bfloat16)
            return 0

        lax.fori_loop(0, weights.shape[0], one_channel, 0, unroll=True)

    for q in range(4):
        pl.when(q_here == q)(functools.partial(run, orders[q]))


def partial_beams(blocks, weights):
    _, chans, snaps, sensors = blocks[0].shape
    beams = weights.shape[2] // 2
    shape = (chans // 2, 2, 4 * snaps, beams)
    return pl.pallas_call(
        beams_kernel,
        out_shape=[
            jax.ShapeDtypeStruct(shape, jnp.float32),
            jax.ShapeDtypeStruct(shape, jnp.bfloat16),
        ],
        in_specs=[pl.BlockSpec(memory_space=pltpu.VMEM)] * (len(blocks) + 1),
        out_specs=[pl.BlockSpec(memory_space=pltpu.VMEM)] * 2,
        compiler_params=pltpu.CompilerParams(vmem_limit_bytes=32 * 2**20),
        name="beams",
    )(*blocks, weights)


def gram_kernel(mine, other, out):
    q, core = lax.axis_index("q"), lax.axis_index("core")
    snaps = mine.shape[2]
    whole = []
    for part in range(2):
        blocks = []
        for b in range(4):
            ours = mine[b, 0].astype(jnp.float32) + mine[b, 1].astype(jnp.float32)
            theirs = other[b, 0].astype(jnp.float32) + other[b, 1].astype(jnp.float32)
            blocks.append(jnp.where(core == part, ours, theirs))
        whole.append(blocks)
    real_y, imag_y = whole

    def row(a):
        low = jnp.where(q % 2 == 0, a[0], a[1])
        high = jnp.where(q % 2 == 0, a[2], a[3])
        return jnp.where(q < 2, low, high)

    def columns(a):
        return jnp.concatenate(
            [jnp.where(core == 0, a[0], a[2]), jnp.where(core == 0, a[1], a[3])], axis=1
        )

    left_real, left_imag = row(real_y), row(imag_y)
    right = jnp.concatenate([columns(real_y), columns(imag_y)], axis=0)
    inverse = 1.0 / snaps

    def halves(a):
        high = a.astype(jnp.bfloat16)
        return high, (a - high.astype(jnp.float32)).astype(jnp.bfloat16)

    right_high, right_low = halves(right)
    rights = jnp.concatenate([right_high, right_low, right_high], axis=0)

    def contract(left):
        high, low = halves(left)
        return lax.dot_general(
            jnp.concatenate([high, high, low], axis=0),
            rights,
            (((0,), (0,)), ((), ())),
            preferred_element_type=jnp.float32,
        )

    out[0, 0] = contract(jnp.concatenate([left_real, left_imag], axis=0)) * inverse
    out[1, 0] = contract(jnp.concatenate([left_imag, -left_real], axis=0)) * inverse


def gram(mine, other):
    beams = mine.shape[3]
    return pl.pallas_call(
        gram_kernel,
        out_shape=jax.ShapeDtypeStruct((2, 1, beams, 2 * beams), jnp.float32),
        in_specs=[pl.BlockSpec(memory_space=pltpu.VMEM)] * 2,
        out_specs=pl.BlockSpec(memory_space=pltpu.VMEM),
        compiler_params=pltpu.CompilerParams(vmem_limit_bytes=32 * 2**20),
        name="gram",
    )(mine, other)


def local(samples, weights, chosen_frequency_bins):
    chans = chosen_frequency_bins.shape[0]
    bins = pltpu.with_memory_space_constraint(chosen_frequency_bins, pltpu.HBM)
    samples = pltpu.with_memory_space_constraint(samples, pltpu.HBM)
    own = [spectra_of(samples, bins, part, 2) for part in range(2)]
    own = [x.reshape(2, chans, *x.shape[1:]) for x in own]

    def pass_on(pieces, pairs):
        return [lax.ppermute(x, "q", pairs) for x in pieces]

    def after(piece, other):
        return lax.optimization_barrier((piece, other))[0]

    far = pass_on(own, FAR)
    near = pass_on(own, NEAR)
    out = pass_on(far, OUT)
    middle = pass_on([after(x, far[0]) for x in own], MIDDLE)
    weights = load(after(weights, far[-1]))
    blocks = own + near + far + middle + out
    keep, send = partial_beams(blocks, weights)
    theirs = lax.ppermute(send, "core", SWAP)
    mine = (keep + theirs.astype(jnp.float32)).astype(jnp.bfloat16)
    mine = lax.all_to_all(mine, ("y", "x"), 0, 0)
    mine = jnp.sum(mine.astype(jnp.float32), axis=0).astype(jnp.bfloat16)
    mine = jnp.broadcast_to(mine[None], (4, 2, *mine.shape[1:]))
    mine = mine.reshape(8, *mine.shape[2:])
    mine = lax.all_to_all(mine, ("q", "zh"), 0, 0)
    mine = mine.reshape(4, 2, *mine.shape[1:])
    other = lax.ppermute(mine, "core", SWAP)
    return gram(mine, other)


def solution(mesh):
    fine = Mesh(mesh.devices.reshape(4, 2, 4, 2, 4), AXES)
    sens = ("y", "zh", "x", "core")
    return jax.shard_map(
        local,
        mesh=fine,
        in_specs=(P(sens, "q", None), P(None, None, sens, "q"), P()),
        out_specs=P(None, sens, "q", None),
        check_vma=False,
    )
```
